32 devices in a mesh: dp: 4 (over x, core), ctx: 2 (over y), tp: 4 (over z).
Axes of the slice: x: 2, y: 2, z: 4, core: 2. Of those that a mesh axis runs over, the one named last changes fastest.
Arguments:
- upstream: bfloat16 [1024, 3072], P(('dp', 'ctx'), 'tp'), may hold values from -6 to 6
- router_logits: float32 [1024, 2], P(('dp', 'ctx')), may hold values from -6 to 6
- expert_ids: int32 [1024, 2], P(('dp', 'ctx')), may hold values from 0 to 7, all different within a row; in each aligned block of 128 rows (0 to 127, 128 to 255, ...) at most 36 rows name the same one
- hidden_saved: bfloat16 [288, 65536], P('dp', ('ctx', 'tp')), may hold values from -0.75 to 0.75
- down_weight: bfloat16 [65536, 3072], P(('ctx', 'tp'), 'dp'), may hold values from -0.0625 to 0.0625
Outputs:
- hidden_grad: bfloat16 [288, 65536], P('dp', ('ctx', 'tp'))
- down_grad: bfloat16 [65536, 3072], P(('ctx', 'tp'), 'dp')
- logit_grad: float32 [1024, 2], P(('dp', 'ctx'))
The draws below stay inside these ranges and needn't reach their ends.
Inputs may be any that keep to these rules, and one draw needn't show every extreme that they name: `expert_ids`: the ids of a row differ; in each aligned block of 128 rows (the rows of one device) no expert is named more than 36 times.
All inputs are finite; a program needn't handle non-finite values.
Results may differ from the reference program's by a relative error of at most 0.013.
Values may be sent and summed in bfloat16 or wider, within the bound.
A program may use at most 192 MiB of HBM per device.

```python
import math
import jax
import jax.numpy as jnp
import numpy as np
from jax import lax

D = 3072
FF = 8192
EXPERTS = 8
TOP = 2
TOK_DEV = 128
CAP = 36
SLOTS = 72
TOKENS = 1024
N_DP = 4
N_CTX = 2


def block_levels(stream_key, extent, shards, least, top_value):
    def one(dim, shards_of):
        draws = jax.random.uniform(jax.random.fold_in(jax.random.fold_in(stream_key, 6), dim), (shards_of,), jnp.float32, least / len(shards), top_value / len(shards))
        return jnp.repeat(jnp.exp(draws), extent[dim] // shards_of).reshape((-1,) + (1,) * (len(extent) - dim - 1))

    factor_of = one(*shards[0])
    for cut in shards[1:]:
        factor_of = factor_of * one(*cut)
    return factor_of


def routed_block(key, own, number, rows, number_of, top, reach, slope):
    order = jax.random.permutation(key, number_of)
    crowded, usual = load_shares(number_of, rows * top, reach, slope, True), load_shares(number_of, rows * top, reach, slope, False)
    places = jnp.arange(number_of)

    def named(tallies, turn):
        used = int((tallies > 0).sum())
        fixed = max(1, used // 4)
        shifted = fixed + (places - fixed + turn * (used - fixed)) % max(1, number_of - fixed)
        return jnp.zeros((number_of,), jnp.int32).at[order[jnp.where(places < fixed, places, shifted)]].set(jnp.asarray(tallies, jnp.int32))

    tallies = jnp.where(number % 4 == 0, named(crowded, number // 4), named(usual, number - number // 4 - 1))
    mixed = jax.random.permutation(jax.random.fold_in(own, 3), number_of)
    donor, taker = mixed[0:number_of // 2 * 2:2], mixed[1:number_of // 2 * 2:2]
    room = jnp.minimum(tallies[donor] - 1, reach - tallies[taker]) // 2
    room = jnp.where((donor == order[0]) | (taker == order[0]) | (tallies[taker] == 0), 0, jnp.maximum(room, 0))
    shifted = jax.random.randint(jax.random.fold_in(own, 4), (number_of // 2,), 0, 1 << 20) % (room + 1)
    tallies = tallies.at[donor].add(-shifted).at[taker].add(shifted)
    labels = jnp.searchsorted(jnp.cumsum(tallies), jnp.arange(rows * top), side="right").astype(jnp.int32)
    table = labels.reshape(top, rows).T
    table = table[jax.random.permutation(jax.random.fold_in(own, 1), rows)]
    turn = jax.random.randint(jax.random.fold_in(own, 2), (rows, 1), 0, top)
    return jnp.take_along_axis(table, (jnp.arange(top)[None, :] + turn) % top, axis=1)


def load_shares(amount, total, reach, lean, full):
    loads = [(1 << 20) // math.isqrt(rank ** lean) + 1 for rank in range(1, amount + 1)]
    largest = reach if full else min(reach, max(-(-total // amount), total * loads[0] // sum(loads)))
    least = 1 if total - largest >= amount - 1 else 0
    given, spare = [largest] + [least] * (amount - 1), total - largest - least * (amount - 1)
    while spare > 0:
        candidates = [i for i in range(1, amount) if given[i] < largest] or [i for i in range(1, amount) if given[i] < reach]
        pool, budget = sum([loads[i] for i in candidates]), spare
        for i in candidates:
            more = min(reach - given[i], max(1, budget * loads[i] // pool), spare)
            given[i] = given[i] + more
            spare = spare - more
    return np.array(given)


def noise(stream_key, extent, width, reach, pieces=(), held_as=jnp.bfloat16):
    gain = block_levels(stream_key, extent, pieces, -0.22, 0.18) if pieces else 1.0
    result = jax.random.normal(stream_key, extent, jnp.float32) * width * gain
    return jnp.minimum(jnp.maximum(result, -reach), reach).astype(held_as)


def setup_inputs(seed: int = 0) -> dict:
    arg_keys = jax.random.split(jax.random.key(seed), 6)
    upstream = noise(arg_keys[0], (TOKENS, D), 1.0, 6.0, ((0, 8), (1, 4)))
    router_logits = noise(arg_keys[1], (TOKENS, TOP), 1.0, 6.0, ((0, 8),), jnp.float32)
    expert_ids_keys = jax.random.split(jax.random.fold_in(arg_keys[2], 1), TOKENS // TOK_DEV)
    expert_ids_turns = jax.random.permutation(jax.random.fold_in(arg_keys[2], 3), TOKENS // TOK_DEV)
    expert_ids = jax.vmap(lambda own, number: routed_block(jax.random.fold_in(arg_keys[2], 2), own, number, TOK_DEV, EXPERTS, TOP, CAP, 1))(expert_ids_keys, expert_ids_turns).reshape((TOKENS, TOP))
    hidden_saved = noise(arg_keys[3], (N_DP * SLOTS, EXPERTS * FF), 0.125, 0.75, ((0, 4), (1, 8)))
    down_weight = noise(arg_keys[4], (EXPERTS * FF, D), FF ** -0.5, 0.0625, ((0, 8), (1, 4)))
    return dict(upstream=upstream, router_logits=router_logits, expert_ids=expert_ids, hidden_saved=hidden_saved, down_weight=down_weight)


def reference(upstream, router_logits, expert_ids, hidden_saved, down_weight):
    gates = 1.0 / (1.0 + jnp.exp(router_logits[:, ::-1] - router_logits))
    gates_sent = gates.astype(jnp.bfloat16)
    block_count = N_DP * N_CTX
    slots_all = N_CTX * CAP
    routes = expert_ids.reshape(block_count, TOK_DEV * TOP)
    onehot = (routes[:, :, None] == jnp.arange(EXPERTS, dtype=jnp.int32)[None, None, :]).astype(jnp.int32)
    earlier = jnp.cumsum(onehot, axis=1) - onehot
    slot = jnp.sum(earlier * onehot, axis=2).astype(jnp.int32)
    block_ids = jnp.arange(block_count, dtype=jnp.int32)[:, None]
    sequence = block_ids // N_CTX
    context = block_ids % N_CTX
    position = (((sequence * EXPERTS + routes) * N_CTX + context) * CAP + slot).astype(jnp.int32)
    route_index = (block_ids * (TOK_DEV * TOP) + jnp.arange(TOK_DEV * TOP, dtype=jnp.int32)[None, :]).astype(jnp.int32)
    sentinel = TOKENS * TOP
    table = jnp.full((N_DP * EXPERTS * slots_all,), sentinel, jnp.int32)
    table = table.at[position.reshape(-1)].set(route_index.reshape(-1))
    padded_rows = jnp.concatenate([upstream, jnp.zeros((1, D), jnp.bfloat16)], axis=0)
    padded_gates = jnp.concatenate([gates_sent.reshape(-1), jnp.zeros((1,), jnp.bfloat16)], axis=0)

    def per_expert(expert):
        weight = lax.dynamic_slice_in_dim(down_weight, expert * FF, FF, 0)
        weight_total = jnp.zeros((FF, D), jnp.float32)
        grads = []
        partials = []
        for sequence_id in range(N_DP):
            start = (sequence_id * EXPERTS + expert) * slots_all
            index = lax.dynamic_slice_in_dim(table, start, slots_all, 0)
            rows = padded_rows[index // TOP]
            gate_rows = padded_gates[index].astype(jnp.float32)[:, None]
            proj = lax.dot_general(rows, weight, (((1,), (1,)), ((), ())), preferred_element_type=jnp.float32)
            saved = lax.dynamic_slice_in_dim(
                lax.dynamic_slice_in_dim(hidden_saved, sequence_id * slots_all, slots_all, 0), expert * FF, FF, 1)
            grads.append((gate_rows * proj).astype(jnp.bfloat16))
            weighted = (gate_rows * rows.astype(jnp.float32)).astype(jnp.bfloat16)
            product = lax.dot_general(saved, weighted, (((0,), (0,)), ((), ())), preferred_element_type=jnp.float32)
            weight_total = weight_total + lax.optimization_barrier(product.astype(jnp.bfloat16)).astype(jnp.float32)
            partials.append(jnp.sum(saved.astype(jnp.float32) * proj, axis=1))
        return jnp.stack(grads), weight_total.astype(jnp.bfloat16), jnp.stack(partials)

    grads, weights, partials = lax.map(per_expert, jnp.arange(EXPERTS, dtype=jnp.int32))
    hidden_grad = grads.transpose(1, 2, 0, 3).reshape(N_DP * slots_all, EXPERTS * FF)
    down_grad = weights.reshape(EXPERTS * FF, D)
    flat_parts = partials.transpose(1, 0, 2).reshape(-1)
    route_grad = jnp.zeros((sentinel + 1,), jnp.float32).at[table].add(flat_parts)
    route_grad = route_grad[:sentinel].reshape(TOKENS, TOP)
    logit_grad = gates * (route_grad - jnp.sum(gates * route_grad, axis=1, keepdims=True))
    return hidden_grad, down_grad, logit_grad
```

```python
import jax
import jax.numpy as jnp
from jax import lax
from jax.sharding import PartitionSpec as P

EXPERTS = 8
TOP = 2


def swap(value, distance):
    count = lax.axis_size("dp")
    return lax.ppermute(value, "dp", [(i, i ^ distance) for i in range(count)])


def local(upstream, router_logits, expert_ids, hidden_saved, down_weight):
    token_count, feature_cols = upstream.shape
    dp_count = lax.axis_size("dp")
    tensor_count = lax.axis_size("tp")
    context_count = lax.axis_size("ctx")
    block_count = context_count * tensor_count
    slots = hidden_saved.shape[0]
    capacity = slots // context_count
    group_size = block_count // EXPERTS
    own_cols = down_weight.shape[1]
    me = lax.axis_index("dp")

    saved_cross = swap(hidden_saved, 2)
    saved_near = swap(hidden_saved, 1)

    gates = 1.0 / (1.0 + jnp.exp(router_logits[:, ::-1] - router_logits))
    gates_sent = gates.astype(jnp.bfloat16)
    routes = expert_ids.reshape(-1)
    onehot = routes[:, None] == jnp.arange(EXPERTS, dtype=jnp.int32)[None, :]
    number = jnp.arange(token_count * TOP, dtype=jnp.int32)
    earlier = lax.dot_general(
        (number[:, None] > number[None, :]).astype(jnp.bfloat16),
        onehot.astype(jnp.bfloat16),
        (((1,), (0,)), ((), ())),
        preferred_element_type=jnp.float32,
    )
    slot = jnp.sum(jnp.where(onehot, earlier, 0.0), axis=1).astype(jnp.int32)
    position = routes * capacity + slot
    place = (position[:, None] == jnp.arange(EXPERTS * capacity, dtype=jnp.int32)[None, :]).astype(
        jnp.float32
    )
    token_place = (
        place.reshape(token_count, TOP, EXPERTS * capacity).sum(axis=1).astype(jnp.bfloat16)
    )
    gate_packed = jnp.sum(
        place * gates_sent.reshape(-1).astype(jnp.float32)[:, None], axis=0
    ).astype(jnp.bfloat16)
    packed = lax.dot_general(
        token_place, upstream, (((0,), (0,)), ((), ())), preferred_element_type=jnp.float32
    ).astype(jnp.bfloat16)

    def spread(value):
        width = value.shape[-1]
        return jnp.broadcast_to(
            value.reshape(EXPERTS, 1, capacity, width), (EXPERTS, group_size, capacity, width)
        ).reshape(block_count, capacity, width)

    received = lax.all_to_all(spread(packed), ("ctx", "tp"), split_axis=0, concat_axis=0, tiled=True)
    gate_in = lax.all_to_all(
        spread(gate_packed[:, None]), ("ctx", "tp"), split_axis=0, concat_axis=0, tiled=True
    )
    rows = received.reshape(context_count, tensor_count, capacity, feature_cols)
    rows = rows.transpose(0, 2, 1, 3).reshape(slots, tensor_count * feature_cols)
    gate_own = gate_in.reshape(context_count, tensor_count, capacity)[:, 0, :].reshape(slots)
    rows = rows.reshape(slots, dp_count, own_cols).transpose(1, 0, 2)
    rows = lax.all_to_all(rows, "dp", split_axis=0, concat_axis=0, tiled=True)
    gate_all = lax.all_gather(gate_own, "dp")

    def ordered(value):
        return [lax.dynamic_index_in_dim(value, me ^ m, 0, keepdims=False) for m in range(4)]

    rows = ordered(rows)
    gate_rows = jnp.concatenate(ordered(gate_all)).astype(jnp.float32)[:, None]

    def project(value):
        return lax.dot_general(
            value, down_weight, (((1,), (1,)), ((), ())), preferred_element_type=jnp.float32
        )

    far = project(jnp.concatenate(rows[2:])).astype(jnp.bfloat16)
    far_near = swap(far[slots:], 1)
    far_sum = (far[:slots].astype(jnp.float32) + far_near.astype(jnp.float32)).astype(jnp.bfloat16)
    cross = swap(far_sum, 2)

    near = project(jnp.concatenate(rows[:2])).astype(jnp.bfloat16)
    near_in = swap(near[slots:], 1)

    saved_far = swap(saved_cross, 1)
    saved = jnp.concatenate([hidden_saved, saved_near, saved_cross, saved_far])
    weighted = (gate_rows * jnp.concatenate(rows).astype(jnp.float32)).astype(jnp.bfloat16)
    down_grad = lax.dot_general(
        saved, weighted, (((0,), (0,)), ((), ())), preferred_element_type=jnp.float32
    ).astype(jnp.bfloat16)

    def parts(left, right):
        return jnp.sum(left.astype(jnp.float32) * right.astype(jnp.float32), axis=1)

    part = jnp.stack(
        [
            parts(hidden_saved, near[:slots]),
            parts(saved_near, near[slots:]),
            parts(saved_cross, far[:slots]),
            parts(saved_far, far[slots:]),
        ]
    )
    part = jnp.stack([lax.dynamic_index_in_dim(part, me ^ m, 0, keepdims=False) for m in range(4)])
    every = lax.all_gather(part, ("dp", "ctx", "tp"))
    every = every.reshape(dp_count, EXPERTS, group_size, dp_count, context_count, capacity)
    mine = lax.dynamic_index_in_dim(every, me, 3, keepdims=False)
    mine = lax.dynamic_index_in_dim(mine, lax.axis_index("ctx"), 3, keepdims=False)
    expert_sums = mine.sum(axis=(0, 2)).reshape(-1)
    route_grad = jnp.sum(place * expert_sums[None, :], axis=1).reshape(token_count, TOP)
    logit_grad = gates * (route_grad - jnp.sum(gates * route_grad, axis=1, keepdims=True))

    proj = (
        near[:slots].astype(jnp.float32) + near_in.astype(jnp.float32) + cross.astype(jnp.float32)
    )
    hidden_grad = (gate_own.astype(jnp.float32)[:, None] * proj).astype(jnp.bfloat16)
    return (hidden_grad, down_grad, logit_grad)


def solution(mesh):
    in_specs = (
        P(("dp", "ctx"), "tp"),
        P(("dp", "ctx"), None),
        P(("dp", "ctx"), None),
        P("dp", ("ctx", "tp")),
        P(("ctx", "tp"), "dp"),
    )
    out_specs = (P("dp", ("ctx", "tp")), P(("ctx", "tp"), "dp"), P(("dp", "ctx"), None))
    return jax.shard_map(local, mesh=mesh, in_specs=in_specs, out_specs=out_specs, check_vma=False)
```

```python
import functools

import jax
import jax.numpy as jnp
from jax import lax
from jax.experimental import pallas as pl
from jax.experimental.pallas import tpu as pltpu
from jax.sharding import PartitionSpec as P

EXPERTS = 8
TOP = 2
LANES = 128
MESH = pl.DeviceIdType.MESH


def swap(value, distance):
    count = lax.axis_size("dp")
    return lax.ppermute(value, "dp", [(i, i ^ distance) for i in range(count)])


def exchange(
    sizes,
    packed,
    pick,
    pick_gate,
    slot_lane,
    saved_in,
    weight_in,
    far_sum,
    near_sum,
    saved,
    weighted,
    gate_out,
    part,
    recv,
    weight,
    rows,
    far_own,
    far_stage,
    near_stage,
    far_in,
    near_in,
    disp_send,
    disp_recv,
    cross_send,
    cross_recv,
    core_send,
    core_recv,
    pass_send,
    pass_recv,
    far_send,
    far_recv,
    near_send,
    near_recv,
    weight_sem,
    own_sem,
):
    dp_count, context_count, tensor_count, group_size = sizes
    block_count = context_count * tensor_count
    source_count = dp_count * context_count
    slots = saved.shape[1]
    hidden = saved.shape[2]
    width = min(1024, hidden)
    chunks = hidden // width
    pad = packed.shape[1]
    me = lax.axis_index("dp")
    ctx = lax.axis_index("ctx")
    tp = lax.axis_index("tp")
    mate = me + 1 - 2 * (me % 2)
    cross = me + 2 - 4 * ((me // 2) % 2)
    order = (me, mate, cross, cross + 1 - 2 * (cross % 2))
    block = ctx * tensor_count + tp
    source = me * context_count + ctx
    to_self = tp == me

    def piece(k):
        return pl.ds(pl.multiple_of(k * width, width), width)

    def load(k):
        return pltpu.make_async_copy(
            weight_in.at[piece(k), :], weight.at[piece(k), :], weight_sem.at[k]
        )

    own = pltpu.make_async_copy(saved_in, saved.at[0], own_sem)

    @pl.loop(0, chunks)
    def _(k):
        load(k).start()

    own.start()

    barrier = pltpu.get_barrier_semaphore()

    @pl.loop(0, source_count)
    def _(n):
        @pl.when(jnp.logical_not(to_self & (n == source)))
        def _():
            pl.semaphore_signal(
                barrier,
                inc=1,
                device_id=(n // context_count, n % context_count, me),
                device_id_type=MESH,
            )

    for other in (mate, cross):
        pl.semaphore_signal(barrier, inc=1, device_id=(other, ctx, tp), device_id_type=MESH)

    @pl.when(to_self)
    def _():
        pl.semaphore_wait(barrier, block_count + 1)

    @pl.when(jnp.logical_not(to_self))
    def _():
        pl.semaphore_wait(barrier, block_count + 2)

    def dispatch(b):
        return pltpu.make_async_remote_copy(
            src_ref=packed.at[b // group_size],
            dst_ref=recv.at[source],
            send_sem=disp_send.at[b],
            recv_sem=disp_recv.at[source],
            device_id=(tp, b // tensor_count, b % tensor_count),
            device_id_type=MESH,
        )

    def arrival(n):
        return pltpu.make_async_remote_copy(
            src_ref=packed.at[0],
            dst_ref=recv.at[n],
            send_sem=disp_send.at[0],
            recv_sem=disp_recv.at[n],
            device_id=(tp, ctx, tp),
            device_id_type=MESH,
        )

    def remote(src, dst, send, recv_sem, k, device):
        return pltpu.make_async_remote_copy(
            src_ref=src,
            dst_ref=dst,
            send_sem=send.at[k],
            recv_sem=recv_sem.at[k],
            device_id=(device, ctx, tp),
            device_id_type=MESH,
        )

    def to_cross(k):
        return remote(
            saved_in.at[:, piece(k)], saved.at[2, :, piece(k)], cross_send, cross_recv, k, cross
        )

    def to_core(k):
        return remote(
            saved_in.at[:, piece(k)], saved.at[1, :, piece(k)], core_send, core_recv, k, mate
        )

    def pass_on(k):
        return remote(
            saved.at[2, :, piece(k)], saved.at[3, :, piece(k)], pass_send, pass_recv, k, mate
        )

    def send_far(k):
        return remote(
            far_stage.at[:, piece(k)], far_in.at[:, piece(k)], far_send, far_recv, k, mate
        )

    def send_near(k):
        return remote(
            near_stage.at[:, piece(k)], near_in.at[:, piece(k)], near_send, near_recv, k, mate
        )

    @pl.loop(0, block_count)
    def _(b):
        @pl.when(jnp.logical_not(to_self & (b == block)))
        def _():
            dispatch(b).start()

    @pl.loop(0, chunks)
    def _(k):
        to_cross(k).start()

    @pl.loop(0, chunks)
    def _(k):
        to_core(k).start()

    @pl.when(to_self)
    def _():
        recv[source] = packed[block // group_size]

    part[...] = jnp.zeros_like(part)

    @pl.loop(0, source_count)
    def _(n):
        @pl.when(jnp.logical_not(to_self & (n == source)))
        def _():
            arrival(n).wait_recv()

    placed, gate_columns = [], []
    for sequence in order:
        found = recv[pl.ds(sequence * context_count, context_count)]
        found = found.reshape(context_count * pad, found.shape[2])
        placed.append(jnp.dot(pick[...], found, preferred_element_type=jnp.float32))
        gate_lanes = jnp.dot(
            pick_gate[...], found[:, :LANES], preferred_element_type=jnp.float32
        )
        gate_columns.append(jnp.sum(gate_lanes * slot_lane[...], axis=1, keepdims=True))
    row_values = jnp.concatenate(placed, axis=0)
    gate_column = jnp.concatenate(gate_columns, axis=0)
    rows[...] = row_values.astype(jnp.bfloat16)
    weighted[...] = (gate_column * row_values).astype(jnp.bfloat16)
    gate_out[...] = jnp.broadcast_to(gate_columns[0], gate_out.shape)

    @pl.loop(0, chunks)
    def _(k):
        load(k).wait()
        proj = lax.dot_general(
            rows[...],
            weight[piece(k), :],
            (((1,), (1,)), ((), ())),
            preferred_element_type=jnp.float32,
        )
        near_sum[:, piece(k)] = proj[:slots]
        near_stage[:, piece(k)] = proj[slots : 2 * slots].astype(jnp.bfloat16)
        far_own[:, piece(k)] = proj[2 * slots : 3 * slots]
        far_stage[:, piece(k)] = proj[3 * slots :].astype(jnp.bfloat16)
        send_far(k).start()
        send_near(k).start()

    own.wait()

    def tally(m, left, right):
        product = left.astype(jnp.float32) * right.astype(jnp.float32)
        total = product[:, :LANES]
        for j in range(1, width // LANES):
            total = total + product[:, j * LANES : (j + 1) * LANES]
        part[m] += total

    @pl.loop(0, chunks)
    def _(k):
        to_cross(k).wait_recv()
        pass_on(k).start()
        to_core(k).wait_recv()
        tally(0, saved[0, :, piece(k)], near_sum[:, piece(k)])
        tally(1, saved[1, :, piece(k)], near_stage[:, piece(k)])
        tally(2, saved[2, :, piece(k)], far_own[:, piece(k)])
        send_far(k).wait_recv()
        far_sum[:, piece(k)] = (
            far_own[:, piece(k)] + far_in[:, piece(k)].astype(jnp.float32)
        ).astype(jnp.bfloat16)
        send_near(k).wait_recv()
        near_sum[:, piece(k)] += near_in[:, piece(k)].astype(jnp.float32)

    @pl.loop(0, chunks)
    def _(k):
        pass_on(k).wait_recv()
        tally(3, saved[3, :, piece(k)], far_stage[:, piece(k)])

    @pl.loop(0, chunks)
    def _(k):
        to_cross(k).wait_send()
        to_core(k).wait_send()
        pass_on(k).wait_send()
        send_far(k).wait_send()
        send_near(k).wait_send()

    @pl.loop(0, block_count)
    def _(b):
        @pl.when(jnp.logical_not(to_self & (b == block)))
        def _():
            dispatch(b).wait_send()


def run_exchange(packed, pick, pick_gate, slot_lane, hidden_saved, down_weight):
    dp_count = lax.axis_size("dp")
    context_count = lax.axis_size("ctx")
    tensor_count = lax.axis_size("tp")
    block_count = context_count * tensor_count
    slots, hidden = hidden_saved.shape
    cols = down_weight.shape[1]
    chunks = hidden // min(1024, hidden)
    bf16, f32 = jnp.bfloat16, jnp.float32
    vmem = pl.BlockSpec(memory_space=pltpu.VMEM)
    dma = pltpu.SemaphoreType.DMA
    return pl.pallas_call(
        functools.partial(
            exchange, (dp_count, context_count, tensor_count, block_count // EXPERTS)
        ),
        out_shape=[
            jax.ShapeDtypeStruct((slots, hidden), bf16),
            jax.ShapeDtypeStruct((slots, hidden), f32),
            jax.ShapeDtypeStruct((4, slots, hidden), bf16),
            jax.ShapeDtypeStruct((4 * slots, cols), bf16),
            jax.ShapeDtypeStruct((slots, LANES), f32),
            jax.ShapeDtypeStruct((4, slots, LANES), f32),
        ],
        in_specs=[vmem] * 4 + [pl.BlockSpec(memory_space=pl.ANY)] * 2,
        out_specs=[vmem] * 6,
        scratch_shapes=[
            pltpu.VMEM((dp_count * context_count,) + packed.shape[1:], bf16),
            pltpu.VMEM((hidden, cols), bf16),
            pltpu.VMEM((4 * slots, cols), bf16),
            pltpu.VMEM((slots, hidden), f32),
            pltpu.VMEM((slots, hidden), bf16),
            pltpu.VMEM((slots, hidden), bf16),
            pltpu.VMEM((slots, hidden), bf16),
            pltpu.VMEM((slots, hidden), bf16),
            dma((block_count,)),
            dma((dp_count * context_count,)),
        ]
        + [dma((chunks,))] * 11
        + [dma],
        compiler_params=pltpu.CompilerParams(
            collective_id=0, has_side_effects=True, vmem_limit_bytes=56 * 1024 * 1024
        ),
        cost_estimate=pl.CostEstimate(
            flops=8 * slots * hidden * cols, bytes_accessed=2 * hidden * cols, transcendentals=0
        ),
    )(packed, pick, pick_gate, slot_lane, hidden_saved, down_weight)


def local(upstream, router_logits, expert_ids, hidden_saved, down_weight):
    token_count, feature_cols = upstream.shape
    dp_count = lax.axis_size("dp")
    tensor_count = lax.axis_size("tp")
    context_count = lax.axis_size("ctx")
    block_count = context_count * tensor_count
    slots = hidden_saved.shape[0]
    capacity = slots // context_count
    group_size = block_count // EXPERTS
    pad = -(-(capacity + 1) // 16) * 16
    me = lax.axis_index("dp")
    assert dp_count == 4 and tensor_count == dp_count and capacity <= LANES

    gates = 1.0 / (1.0 + jnp.exp(router_logits[:, ::-1] - router_logits))
    gates_sent = gates.astype(jnp.bfloat16)
    routes = expert_ids.reshape(-1)
    onehot = routes[:, None] == jnp.arange(EXPERTS, dtype=jnp.int32)[None, :]
    number = jnp.arange(token_count * TOP, dtype=jnp.int32)
    earlier = lax.dot_general(
        (number[:, None] > number[None, :]).astype(jnp.bfloat16),
        onehot.astype(jnp.bfloat16),
        (((1,), (0,)), ((), ())),
        preferred_element_type=jnp.float32,
    )
    slot = jnp.sum(jnp.where(onehot, earlier, 0.0), axis=1).astype(jnp.int32)
    position = routes * pad + slot
    place = (position[:, None] == jnp.arange(EXPERTS * pad, dtype=jnp.int32)[None, :]).astype(
        jnp.float32
    )
    token_place = place.reshape(token_count, TOP, EXPERTS * pad).sum(axis=1).astype(jnp.bfloat16)
    gate_packed = jnp.sum(place * gates_sent.reshape(-1).astype(jnp.float32)[:, None], axis=0)
    packed = lax.dot_general(
        token_place, upstream, (((0,), (0,)), ((), ())), preferred_element_type=jnp.float32
    ).reshape(EXPERTS, pad, feature_cols)
    gate_line = jnp.pad(
        gate_packed.reshape(EXPERTS, 1, pad), ((0, 0), (0, 0), (0, feature_cols - pad))
    )
    line = jnp.arange(pad, dtype=jnp.int32)[None, :, None]
    packed = jnp.where(line == capacity, gate_line, packed).astype(jnp.bfloat16)

    index = jnp.arange(slots, dtype=jnp.int32)
    first = (index // capacity) * pad
    columns = jnp.arange(context_count * pad, dtype=jnp.int32)[None, :]
    pick = ((first + index % capacity)[:, None] == columns).astype(jnp.bfloat16)
    pick_gate = ((first + capacity)[:, None] == columns).astype(jnp.bfloat16)
    slot_lane = (
        (index % capacity)[:, None] == jnp.arange(LANES, dtype=jnp.int32)[None, :]
    ).astype(jnp.float32)

    far_sum, near_sum, saved, weighted, gate_own, part = run_exchange(
        packed, pick, pick_gate, slot_lane, hidden_saved, down_weight
    )
    cross = swap(far_sum, 2)

    part = part.sum(axis=2)
    order = jnp.stack([me ^ m for m in range(4)])
    part = jnp.stack([jnp.sum(jnp.where((order == s)[:, None], part, 0.0), 0) for s in range(4)])
    part = lax.all_to_all(part, "dp", split_axis=0, concat_axis=0, tiled=True).sum(axis=0)
    outgoing = jnp.broadcast_to(
        part.reshape(context_count, 1, capacity), (context_count, tensor_count, capacity)
    ).reshape(block_count, capacity)
    returned = lax.all_to_all(outgoing, ("ctx", "tp"), split_axis=0, concat_axis=0, tiled=True)
    expert_sums = returned.reshape(EXPERTS, group_size, capacity).sum(axis=1)
    expert_sums = jnp.pad(expert_sums, ((0, 0), (0, pad - capacity))).reshape(-1)
    route_grad = jnp.sum(place * expert_sums[None, :], axis=1).reshape(token_count, TOP)
    logit_grad = gates * (route_grad - jnp.sum(gates * route_grad, axis=1, keepdims=True))

    down_grad = lax.dot_general(
        saved.reshape(4 * slots, -1),
        weighted,
        (((0,), (0,)), ((), ())),
        preferred_element_type=jnp.float32,
    ).astype(jnp.bfloat16)

    proj = near_sum + cross.astype(jnp.float32)
    hidden_grad = (gate_own[:, :1] * proj).astype(jnp.bfloat16)
    return (hidden_grad, down_grad, logit_grad)


def solution(mesh):
    in_specs = (
        P(("dp", "ctx"), "tp"),
        P(("dp", "ctx"), None),
        P(("dp", "ctx"), None),
        P("dp", ("ctx", "tp")),
        P(("ctx", "tp"), "dp"),
    )
    out_specs = (P("dp", ("ctx", "tp")), P(("ctx", "tp"), "dp"), P(("dp", "ctx"), None))
    return jax.shard_map(local, mesh=mesh, in_specs=in_specs, out_specs=out_specs, check_vma=False)
```

```python
import functools

import jax
import jax.numpy as jnp
import numpy as np
from jax import lax
from jax.experimental import pallas as pl
from jax.experimental.pallas import tpu as pltpu
from jax.sharding import PartitionSpec as P

EXPERTS = 8
TOP = 2
LANES = 128
MESH = pl.DeviceIdType.MESH


def swap(value, distance):
    count = lax.axis_size("dp")
    return lax.ppermute(value, "dp", [(i, i ^ distance) for i in range(count)])


def chunk_width(slots, hidden):
    return min(1024 if slots <= 256 else 128, hidden)


def exchange(
    sizes,
    id_rows,
    logit_rows,
    upstream,
    pick,
    pick_gate,
    slot_lane,
    saved_in,
    weight_in,
    far_sum,
    near_sum,
    saved,
    weighted,
    gate_out,
    part_sum,
    packed,
    recv,
    leaving,
    landing,
    weight,
    rows,
    far_own,
    far_stage,
    near_stage,
    far_in,
    near_in,
    part,
    part_in,
    disp_send,
    disp_recv,
    row_send,
    row_recv,
    part_send,
    part_recv,
    cross_send,
    cross_recv,
    core_send,
    core_recv,
    pass_send,
    pass_recv,
    far_send,
    far_recv,
    near_send,
    near_recv,
    weight_sem,
    own_sem,
):
    context_count, tensor_count, group_size = sizes
    block_count = context_count * tensor_count
    tokens, cols = upstream.shape
    slots = saved.shape[1]
    capacity = slots // context_count
    hidden = saved.shape[2]
    width = chunk_width(slots, hidden)
    chunks = hidden // width
    early = min(3, chunks)
    pad = packed.shape[1]
    me = lax.axis_index("dp")
    ctx = lax.axis_index("ctx")
    tp = lax.axis_index("tp")
    mate = me + 1 - 2 * (me % 2)
    cross = me + 2 - 4 * ((me // 2) % 2)
    order = (me, mate, cross, cross + 1 - 2 * (cross % 2))
    block = ctx * tensor_count + tp

    def piece(k):
        return pl.ds(pl.multiple_of(k * width, width), width)

    def load(k):
        return pltpu.make_async_copy(
            weight_in.at[piece(k), :], weight.at[piece(k), :], weight_sem.at[k]
        )

    own = pltpu.make_async_copy(saved_in, saved.at[0], own_sem)

    barrier = pltpu.get_barrier_semaphore()

    @pl.loop(0, block_count)
    def _(b):
        @pl.when(b != block)
        def _():
            pl.semaphore_signal(
                barrier,
                inc=1,
                device_id=(me, b // tensor_count, b % tensor_count),
                device_id_type=MESH,
            )

    for other in order[1:]:
        pl.semaphore_signal(barrier, inc=1, device_id=(other, ctx, tp), device_id_type=MESH)

    @pl.loop(0, chunks)
    def _(k):
        load(k).start()

    own.start()

    f32, bf16 = jnp.float32, jnp.bfloat16
    token = lax.broadcasted_iota(jnp.int32, (tokens, tokens), 0)
    lane = lax.broadcasted_iota(jnp.int32, (tokens, tokens), 1)
    lane_value = lane.astype(f32)

    def column(line):
        return jnp.sum(jnp.where(token == lane, line, 0.0), axis=1, keepdims=True)

    experts = [column(id_rows[k : k + 1, :].astype(f32)) for k in range(TOP)]
    logits = [column(logit_rows[k : k + 1, :]) for k in range(TOP)]
    gates = [
        (1.0 / (1.0 + jnp.exp(logits[1 - k] - logits[k]))).astype(bf16).astype(f32)
        for k in range(TOP)
    ]
    named = [jnp.where(expert == lane_value, 1.0, 0.0) for expert in experts]
    prior = jnp.dot(
        jnp.where(lane < token, 1.0, 0.0).astype(bf16),
        (named[0] + named[1]).astype(bf16),
        preferred_element_type=f32,
    )
    slot = [jnp.sum(prior * one, axis=1, keepdims=True) for one in named]
    wide = lax.broadcasted_iota(jnp.int32, (tokens, EXPERTS * pad), 1).astype(f32)
    place = sum(
        jnp.where(experts[k] * float(pad) + slot[k] == wide, 1.0, 0.0) for k in range(TOP)
    )
    sorted_rows = lax.dot_general(
        place.astype(bf16), upstream[...], (((0,), (0,)), ((), ())), preferred_element_type=f32
    )
    gate_line = lax.broadcasted_iota(jnp.int32, (pad, LANES), 0) == capacity
    at_slot = [jnp.where(slot[k] == lane_value, gates[k], 0.0) for k in range(TOP)]
    for e in range(EXPERTS):
        line = sum(
            jnp.sum(jnp.where(experts[k] == float(e), at_slot[k], 0.0), axis=0, keepdims=True)
            for k in range(TOP)
        )
        found = sorted_rows[e * pad : (e + 1) * pad]
        packed[e, :, :LANES] = jnp.where(gate_line, line, found[:, :LANES]).astype(bf16)
        packed[e, :, LANES:] = found[:, LANES:].astype(bf16)

    pl.semaphore_wait(barrier, block_count - 1 + len(order) - 1)

    def dispatch(b):
        return pltpu.make_async_remote_copy(
            src_ref=packed.at[b // group_size],
            dst_ref=recv.at[block],
            send_sem=disp_send.at[b],
            recv_sem=disp_recv.at[block],
            device_id=(me, b // tensor_count, b % tensor_count),
            device_id_type=MESH,
        )

    def arrival(b):
        return pltpu.make_async_remote_copy(
            src_ref=packed.at[0],
            dst_ref=recv.at[b],
            send_sem=disp_send.at[0],
            recv_sem=disp_recv.at[b],
            device_id=(me, b // tensor_count, b % tensor_count),
            device_id_type=MESH,
        )

    def remote(src, dst, send, recv_sem, k, device):
        return pltpu.make_async_remote_copy(
            src_ref=src,
            dst_ref=dst,
            send_sem=send.at[k],
            recv_sem=recv_sem.at[k],
            device_id=(device, ctx, tp),
            device_id_type=MESH,
        )

    def to_dp(m):
        return remote(leaving.at[m - 1], landing.at[m], row_send, row_recv, m, order[m])

    def part_to(m):
        return remote(part.at[m], part_in.at[m], part_send, part_recv, m, order[m])

    def to_cross(k):
        return remote(
            saved_in.at[:, piece(k)], saved.at[2, :, piece(k)], cross_send, cross_recv, k, cross
        )

    def to_core(k):
        return remote(
            saved_in.at[:, piece(k)], saved.at[1, :, piece(k)], core_send, core_recv, k, mate
        )

    def pass_on(k):
        return remote(
            saved.at[2, :, piece(k)], saved.at[3, :, piece(k)], pass_send, pass_recv, k, mate
        )

    def send_far(k):
        return remote(
            far_stage.at[:, piece(k)], far_in.at[:, piece(k)], far_send, far_recv, k, mate
        )

    def send_near(k):
        return remote(
            near_stage.at[:, piece(k)], near_in.at[:, piece(k)], near_send, near_recv, k, mate
        )

    @pl.loop(0, block_count)
    def _(b):
        @pl.when(b != block)
        def _():
            dispatch(b).start()

    @pl.loop(0, early)
    def _(k):
        to_cross(k).start()

    recv[block] = packed[block // group_size]
    part[...] = jnp.zeros_like(part)

    @pl.loop(0, block_count)
    def _(b):
        @pl.when(b != block)
        def _():
            arrival(b).wait_recv()

    joined = pick.shape[1] // pad
    spans = [
        (first, pl.ds(first * capacity, joined * capacity))
        for first in range(0, context_count, joined)
    ]

    def block_rows(first, t):
        return jnp.concatenate(
            [recv[(first + c) * tensor_count + t] for c in range(joined)], axis=0
        )

    for first, span in spans:
        gate_lanes = jnp.dot(
            pick_gate[...], block_rows(first, 0)[:, :LANES], preferred_element_type=f32
        )
        gate = jnp.sum(gate_lanes * slot_lane[...], axis=1, keepdims=True)
        gate_out[span, :] = jnp.broadcast_to(gate, (joined * capacity, LANES))
    for m in (3, 2, 1, 0):
        there = leaving.at[m - 1] if m else landing.at[0]
        for first, span in spans:
            value = jnp.dot(pick[...], block_rows(first, order[m]), preferred_element_type=f32)
            there[span, :cols] = value.astype(bf16)
            there[span, cols:] = gate_out[span, :].astype(bf16)
        if m:
            to_dp(m).start()

    @pl.loop(early, chunks)
    def _(k):
        to_cross(k).start()

    @pl.loop(0, chunks)
    def _(k):
        to_core(k).start()

    for m in (1, 2, 3):
        to_dp(m).wait_recv()
    if slots % 16 == 0:
        pieces = [[(m, span)] for m in range(4) for _, span in spans]
    else:
        pieces = [[(m, pl.ds(0, slots)) for m in range(4)]]
    start = 0
    for group in pieces:
        row_values = jnp.concatenate(
            [landing[m, span, :cols].astype(f32) for m, span in group], axis=0
        )
        gate_column = jnp.concatenate(
            [landing[m, span, cols:].astype(f32)[:, :1] for m, span in group], axis=0
        )
        there = pl.ds(start, row_values.shape[0])
        rows[there, :] = row_values.astype(bf16)
        weighted[there, :] = (gate_column * row_values).astype(bf16)
        start += row_values.shape[0]

    @pl.loop(0, chunks)
    def _(k):
        load(k).wait()
        proj = lax.dot_general(
            rows[...],
            weight[piece(k), :],
            (((1,), (1,)), ((), ())),
            preferred_element_type=jnp.float32,
        )
        near_sum[:, piece(k)] = proj[:slots].astype(jnp.bfloat16)
        near_stage[:, piece(k)] = proj[slots : 2 * slots].astype(jnp.bfloat16)
        far_own[:, piece(k)] = proj[2 * slots : 3 * slots].astype(jnp.bfloat16)
        far_stage[:, piece(k)] = proj[3 * slots :].astype(jnp.bfloat16)
        send_far(k).start()
        send_near(k).start()

    own.wait()

    def tally(m, left, right):
        product = left.astype(jnp.float32) * right.astype(jnp.float32)
        total = product[:, :LANES]
        for j in range(1, width // LANES):
            total = total + product[:, j * LANES : (j + 1) * LANES]
        part[m] += total

    @pl.loop(0, chunks)
    def _(k):
        to_cross(k).wait_recv()
        pass_on(k).start()
        to_core(k).wait_recv()
        tally(0, saved[0, :, piece(k)], near_sum[:, piece(k)])
        tally(1, saved[1, :, piece(k)], near_stage[:, piece(k)])
        tally(2, saved[2, :, piece(k)], far_own[:, piece(k)])
        send_far(k).wait_recv()
        far_sum[:, piece(k)] = (
            far_own[:, piece(k)].astype(jnp.float32) + far_in[:, piece(k)].astype(jnp.float32)
        ).astype(jnp.bfloat16)
        send_near(k).wait_recv()
        near_sum[:, piece(k)] = (
            near_sum[:, piece(k)].astype(jnp.float32) + near_in[:, piece(k)].astype(jnp.float32)
        ).astype(jnp.bfloat16)

    @pl.loop(0, chunks)
    def _(k):
        pass_on(k).wait_recv()
        tally(3, saved[3, :, piece(k)], far_stage[:, piece(k)])

    for m in (1, 2, 3):
        part_to(m).start()

    @pl.loop(0, chunks)
    def _(k):
        to_cross(k).wait_send()
        to_core(k).wait_send()
        pass_on(k).wait_send()
        send_far(k).wait_send()
        send_near(k).wait_send()

    @pl.loop(0, block_count)
    def _(b):
        @pl.when(b != block)
        def _():
            dispatch(b).wait_send()

    for m in (1, 2, 3):
        to_dp(m).wait_send()
    for m in (1, 2, 3):
        part_to(m).wait_recv()
    part_sum[...] = (part[0] + part_in[1]) + (part_in[2] + part_in[3])
    for m in (1, 2, 3):
        part_to(m).wait_send()


def run_exchange(
    pad, id_rows, logit_rows, upstream, pick, pick_gate, slot_lane, hidden_saved, down_weight
):
    context_count = lax.axis_size("ctx")
    tensor_count = lax.axis_size("tp")
    block_count = context_count * tensor_count
    slots, hidden = hidden_saved.shape
    cols = down_weight.shape[1]
    chunks = hidden // chunk_width(slots, hidden)
    bf16, f32 = jnp.bfloat16, jnp.float32
    vmem = pl.BlockSpec(memory_space=pltpu.VMEM)
    dma = pltpu.SemaphoreType.DMA
    return pl.pallas_call(
        functools.partial(
            exchange, (context_count, tensor_count, block_count // EXPERTS)
        ),
        out_shape=[
            jax.ShapeDtypeStruct((slots, hidden), bf16),
            jax.ShapeDtypeStruct((slots, hidden), bf16),
            jax.ShapeDtypeStruct((4, slots, hidden), bf16),
            jax.ShapeDtypeStruct((4 * slots, cols), bf16),
            jax.ShapeDtypeStruct((slots, LANES), f32),
            jax.ShapeDtypeStruct((slots, LANES), f32),
        ],
        in_specs=[vmem] * 6 + [pl.BlockSpec(memory_space=pl.ANY)] * 2,
        out_specs=[vmem] * 6,
        scratch_shapes=[
            pltpu.VMEM((EXPERTS, pad, cols), bf16),
            pltpu.VMEM((block_count, pad, cols), bf16),
            pltpu.VMEM((3, slots, cols + LANES), bf16),
            pltpu.VMEM((4, slots, cols + LANES), bf16),
            pltpu.VMEM((hidden, cols), bf16),
            pltpu.VMEM((4 * slots, cols), bf16),
            pltpu.VMEM((slots, hidden), bf16),
            pltpu.VMEM((slots, hidden), bf16),
            pltpu.VMEM((slots, hidden), bf16),
            pltpu.VMEM((slots, hidden), bf16),
            pltpu.VMEM((slots, hidden), bf16),
            pltpu.VMEM((4, slots, LANES), f32),
            pltpu.VMEM((4, slots, LANES), f32),
            dma((block_count,)),
            dma((block_count,)),
            dma((4,)),
            dma((4,)),
            dma((4,)),
            dma((4,)),
        ]
        + [dma((chunks,))] * 11
        + [dma],
        compiler_params=pltpu.CompilerParams(
            collective_id=0, has_side_effects=True, vmem_limit_bytes=60 * 1024 * 1024
        ),
        cost_estimate=pl.CostEstimate(
            flops=8 * slots * hidden * cols, bytes_accessed=2 * hidden * cols, transcendentals=0
        ),
    )(id_rows, logit_rows, upstream, pick, pick_gate, slot_lane, hidden_saved, down_weight)


def local(upstream, router_logits, expert_ids, hidden_saved, down_weight):
    token_count, feature_cols = upstream.shape
    dp_count = lax.axis_size("dp")
    tensor_count = lax.axis_size("tp")
    context_count = lax.axis_size("ctx")
    block_count = context_count * tensor_count
    slots = hidden_saved.shape[0]
    capacity = slots // context_count
    group_size = block_count // EXPERTS
    pad = -(-(capacity + 1) // 16) * 16
    assert dp_count == 4 and tensor_count == dp_count
    assert capacity <= LANES and token_count == LANES

    joined = 4 if context_count % 4 == 0 else context_count
    index = np.arange(joined * capacity)
    first = (index // capacity) * pad
    columns = np.arange(joined * pad)[None, :]
    pick = ((first + index % capacity)[:, None] == columns).astype(jnp.bfloat16)
    pick_gate = ((first + capacity)[:, None] == columns).astype(jnp.bfloat16)
    slot_lane = ((index % capacity)[:, None] == np.arange(LANES)[None, :]).astype(np.float32)

    far_sum, near_sum, saved, weighted, gate_own, part = run_exchange(
        pad,
        expert_ids.T,
        router_logits.T,
        upstream,
        pick,
        pick_gate,
        slot_lane,
        hidden_saved,
        down_weight,
    )
    cross = swap(far_sum, 2)

    part, expert_ids, router_logits = lax.optimization_barrier((part, expert_ids, router_logits))
    part = part.sum(axis=1)
    outgoing = jnp.broadcast_to(
        part.reshape(context_count, 1, capacity), (context_count, tensor_count, capacity)
    ).reshape(block_count, capacity)
    returned = lax.all_to_all(outgoing, ("ctx", "tp"), split_axis=0, concat_axis=0, tiled=True)
    expert_sums = returned.reshape(EXPERTS, group_size, capacity).sum(axis=1)
    gates = 1.0 / (1.0 + jnp.exp(router_logits[:, ::-1] - router_logits))
    onehot = (expert_ids[:, :, None] == jnp.arange(EXPERTS, dtype=jnp.int32)).astype(jnp.float32)
    number = jnp.arange(token_count, dtype=jnp.int32)
    prior = lax.dot_general(
        (number[:, None] > number[None, :]).astype(jnp.bfloat16),
        onehot.sum(axis=1).astype(jnp.bfloat16),
        (((1,), (0,)), ((), ())),
        preferred_element_type=jnp.float32,
    )
    slot = jnp.sum(onehot * prior[:, None, :], axis=2).astype(jnp.int32)
    at_slot = slot[:, :, None] == jnp.arange(capacity, dtype=jnp.int32)
    of_route = jnp.sum(onehot[:, :, :, None] * expert_sums[None, None], axis=2)
    route_grad = jnp.sum(jnp.where(at_slot, of_route, 0.0), axis=2)
    logit_grad = gates * (route_grad - jnp.sum(gates * route_grad, axis=1, keepdims=True))

    down_grad = lax.dot_general(
        saved.reshape(4 * slots, -1),
        weighted,
        (((0,), (0,)), ((), ())),
        preferred_element_type=jnp.float32,
    ).astype(jnp.bfloat16)

    proj = near_sum.astype(jnp.float32) + cross.astype(jnp.float32)
    hidden_grad = (gate_own[:, :1] * proj).astype(jnp.bfloat16)
    return (hidden_grad, down_grad, logit_grad)


def solution(mesh):
    in_specs = (
        P(("dp", "ctx"), "tp"),
        P(("dp", "ctx"), None),
        P(("dp", "ctx"), None),
        P("dp", ("ctx", "tp")),
        P(("ctx", "tp"), "dp"),
    )
    out_specs = (P("dp", ("ctx", "tp")), P(("ctx", "tp"), "dp"), P(("dp", "ctx"), None))
    return jax.shard_map(local, mesh=mesh, in_specs=in_specs, out_specs=out_specs, check_vma=False)
```

```python
import functools

import jax
import jax.numpy as jnp
import numpy as np
from jax import lax
from jax.experimental import pallas as pl
from jax.experimental.pallas import tpu as pltpu
from jax.sharding import PartitionSpec as P

EXPERTS = 8
TOP = 2
LANES = 128
MESH = pl.DeviceIdType.MESH


def swap(value, distance):
    count = lax.axis_size("dp")
    return lax.ppermute(value, "dp", [(i, i ^ distance) for i in range(count)])


def chunk_width(slots, hidden):
    return min(1024 if slots <= 256 else 128, hidden)


def head_chunks(chunks):
    return chunks // 4


def exchange(
    sizes,
    id_rows,
    logit_rows,
    upstream,
    pick,
    pick_gate,
    slot_lane,
    saved_in,
    weight_in,
    far_sum,
    near_sum,
    saved,
    weighted,
    gate_out,
    part_sum,
    packed,
    recv,
    leaving,
    landing,
    weight,
    rows,
    far_own,
    far_stage,
    near_stage,
    far_in,
    near_in,
    part,
    part_in,
    far_head,
    cross_head,
    disp_send,
    disp_recv,
    row_send,
    row_recv,
    part_send,
    part_recv,
    head_send,
    head_recv,
    cross_send,
    cross_recv,
    core_send,
    core_recv,
    pass_send,
    pass_recv,
    far_send,
    far_recv,
    near_send,
    near_recv,
    weight_sem,
    own_sem,
):
    context_count, tensor_count, group_size = sizes
    block_count = context_count * tensor_count
    tokens, cols = upstream.shape
    slots = saved.shape[1]
    capacity = slots // context_count
    hidden = saved.shape[2]
    width = chunk_width(slots, hidden)
    chunks = hidden // width
    early = chunks * 5 // 8
    head = head_chunks(chunks)
    head_width = head * width
    pad = packed.shape[1]
    me = lax.axis_index("dp")
    ctx = lax.axis_index("ctx")
    tp = lax.axis_index("tp")
    mate = me + 1 - 2 * (me % 2)
    cross = me + 2 - 4 * ((me // 2) % 2)
    order = (me, mate, cross, cross + 1 - 2 * (cross % 2))
    block = ctx * tensor_count + tp

    def piece(k):
        return pl.ds(pl.multiple_of(k * width, width), width)

    def load(k):
        return pltpu.make_async_copy(
            weight_in.at[piece(k), :], weight.at[piece(k), :], weight_sem.at[k]
        )

    own = pltpu.make_async_copy(saved_in, saved.at[0], own_sem)

    barrier = pltpu.get_barrier_semaphore()

    @pl.loop(0, block_count)
    def _(b):
        @pl.when(b != block)
        def _():
            pl.semaphore_signal(
                barrier,
                inc=1,
                device_id=(me, b // tensor_count, b % tensor_count),
                device_id_type=MESH,
            )

    for other in order[1:]:
        pl.semaphore_signal(barrier, inc=1, device_id=(other, ctx, tp), device_id_type=MESH)

    @pl.loop(0, chunks)
    def _(k):
        load(k).start()

    own.start()

    f32, bf16 = jnp.float32, jnp.bfloat16
    token = lax.broadcasted_iota(jnp.int32, (tokens, tokens), 0)
    lane = lax.broadcasted_iota(jnp.int32, (tokens, tokens), 1)
    lane_value = lane.astype(f32)

    def column(line):
        return jnp.sum(jnp.where(token == lane, line, 0.0), axis=1, keepdims=True)

    experts = [column(id_rows[k : k + 1, :].astype(f32)) for k in range(TOP)]
    logits = [column(logit_rows[k : k + 1, :]) for k in range(TOP)]
    gates = [
        (1.0 / (1.0 + jnp.exp(logits[1 - k] - logits[k]))).astype(bf16).astype(f32)
        for k in range(TOP)
    ]
    named = [jnp.where(expert == lane_value, 1.0, 0.0) for expert in experts]
    prior = jnp.dot(
        jnp.where(lane < token, 1.0, 0.0).astype(bf16),
        (named[0] + named[1]).astype(bf16),
        preferred_element_type=f32,
    )
    slot = [jnp.sum(prior * one, axis=1, keepdims=True) for one in named]
    wide = lax.broadcasted_iota(jnp.int32, (tokens, EXPERTS * pad), 1).astype(f32)
    place = sum(
        jnp.where(experts[k] * float(pad) + slot[k] == wide, 1.0, 0.0) for k in range(TOP)
    )
    sorted_rows = lax.dot_general(
        place.astype(bf16), upstream[...], (((0,), (0,)), ((), ())), preferred_element_type=f32
    )
    gate_line = lax.broadcasted_iota(jnp.int32, (pad, LANES), 0) == capacity
    at_slot = [jnp.where(slot[k] == lane_value, gates[k], 0.0) for k in range(TOP)]
    for e in range(EXPERTS):
        line = sum(
            jnp.sum(jnp.where(experts[k] == float(e), at_slot[k], 0.0), axis=0, keepdims=True)
            for k in range(TOP)
        )
        found = sorted_rows[e * pad : (e + 1) * pad]
        packed[e, :, :LANES] = jnp.where(gate_line, line, found[:, :LANES]).astype(bf16)
        packed[e, :, LANES:] = found[:, LANES:].astype(bf16)

    pl.semaphore_wait(barrier, block_count - 1 + len(order) - 1)

    def dispatch(b):
        return pltpu.make_async_remote_copy(
            src_ref=packed.at[b // group_size],
            dst_ref=recv.at[block],
            send_sem=disp_send.at[b],
            recv_sem=disp_recv.at[block],
            device_id=(me, b // tensor_count, b % tensor_count),
            device_id_type=MESH,
        )

    def arrival(b):
        return pltpu.make_async_remote_copy(
            src_ref=packed.at[0],
            dst_ref=recv.at[b],
            send_sem=disp_send.at[0],
            recv_sem=disp_recv.at[b],
            device_id=(me, b // tensor_count, b % tensor_count),
            device_id_type=MESH,
        )

    def remote(src, dst, send, recv_sem, k, device):
        return pltpu.make_async_remote_copy(
            src_ref=src,
            dst_ref=dst,
            send_sem=send.at[k],
            recv_sem=recv_sem.at[k],
            device_id=(device, ctx, tp),
            device_id_type=MESH,
        )

    def to_dp(m):
        return remote(leaving.at[m - 1], landing.at[m], row_send, row_recv, m, order[m])

    def part_to(m):
        return remote(part.at[m], part_in.at[m], part_send, part_recv, m, order[m])

    def to_cross(k):
        return remote(
            saved_in.at[:, piece(k)], saved.at[2, :, piece(k)], cross_send, cross_recv, k, cross
        )

    def to_core(k):
        return remote(
            saved_in.at[:, piece(k)], saved.at[1, :, piece(k)], core_send, core_recv, k, mate
        )

    def pass_on(k):
        return remote(
            saved.at[2, :, piece(k)], saved.at[3, :, piece(k)], pass_send, pass_recv, k, mate
        )

    def send_far(k):
        return remote(
            far_stage.at[:, piece(k)], far_in.at[:, piece(k)], far_send, far_recv, k, mate
        )

    def send_near(k):
        return remote(
            near_stage.at[:, piece(k)], near_in.at[:, piece(k)], near_send, near_recv, k, mate
        )

    @pl.loop(1, block_count)
    def _(j):
        dispatch((block + j) % block_count).start()

    @pl.loop(0, early)
    def _(k):
        to_cross(k).start()

    recv[block] = packed[block // group_size]
    part[...] = jnp.zeros_like(part)

    @pl.loop(0, block_count)
    def _(b):
        @pl.when(b != block)
        def _():
            arrival(b).wait_recv()

    joined = pick.shape[1] // pad
    spans = [
        (first, pl.ds(first * capacity, joined * capacity))
        for first in range(0, context_count, joined)
    ]

    def block_rows(first, t):
        return jnp.concatenate(
            [recv[(first + c) * tensor_count + t] for c in range(joined)], axis=0
        )

    for first, span in spans:
        gate_lanes = jnp.dot(
            pick_gate[...], block_rows(first, 0)[:, :LANES], preferred_element_type=f32
        )
        gate = jnp.sum(gate_lanes * slot_lane[...], axis=1, keepdims=True)
        gate_out[span, :] = jnp.broadcast_to(gate, (joined * capacity, LANES))
    for m in (3, 2, 1, 0):
        there = leaving.at[m - 1] if m else landing.at[0]
        for first, span in spans:
            value = jnp.dot(pick[...], block_rows(first, order[m]), preferred_element_type=f32)
            there[span, :cols] = value.astype(bf16)
            there[span, cols:] = gate_out[span, :].astype(bf16)
        if m:
            to_dp(m).start()

    @pl.loop(early, chunks)
    def _(k):
        to_cross(k).start()

    @pl.loop(0, chunks)
    def _(k):
        to_core(k).start()

    for m in (1, 2, 3):
        to_dp(m).wait_recv()
    if slots % 16 == 0:
        pieces = [[(m, span)] for m in range(4) for _, span in spans]
    else:
        pieces = [[(m, pl.ds(0, slots)) for m in range(4)]]
    start = 0
    for group in pieces:
        row_values = jnp.concatenate(
            [landing[m, span, :cols].astype(f32) for m, span in group], axis=0
        )
        gate_column = jnp.concatenate(
            [landing[m, span, cols:].astype(f32)[:, :1] for m, span in group], axis=0
        )
        there = pl.ds(start, row_values.shape[0])
        rows[there, :] = row_values.astype(bf16)
        weighted[there, :] = (gate_column * row_values).astype(bf16)
        start += row_values.shape[0]

    @pl.loop(0, chunks)
    def _(k):
        load(k).wait()
        proj = lax.dot_general(
            rows[...],
            weight[piece(k), :],
            (((1,), (1,)), ((), ())),
            preferred_element_type=jnp.float32,
        )
        near_sum[:, piece(k)] = proj[:slots].astype(jnp.bfloat16)
        near_stage[:, piece(k)] = proj[slots : 2 * slots].astype(jnp.bfloat16)
        far_own[:, piece(k)] = proj[2 * slots : 3 * slots].astype(jnp.bfloat16)
        far_stage[:, piece(k)] = proj[3 * slots :].astype(jnp.bfloat16)
        send_far(k).start()
        send_near(k).start()

    def far_total(k):
        return (
            far_own[:, piece(k)].astype(jnp.float32) + far_in[:, piece(k)].astype(jnp.float32)
        ).astype(jnp.bfloat16)

    def to_head(k):
        return remote(
            far_head.at[:, piece(k)], cross_head.at[:, piece(k)], head_send, head_recv, k, cross
        )

    @pl.loop(0, head)
    def _(k):
        send_far(k).wait_recv()
        far_head[:, piece(k)] = far_total(k)
        to_head(k).start()

    own.wait()

    def tally(m, left, right):
        product = left.astype(jnp.float32) * right.astype(jnp.float32)
        total = product[:, :LANES]
        for j in range(1, width // LANES):
            total = total + product[:, j * LANES : (j + 1) * LANES]
        part[m] += total

    @pl.loop(0, chunks)
    def _(k):
        to_cross(k).wait_recv()
        pass_on(k).start()
        to_core(k).wait_recv()
        tally(0, saved[0, :, piece(k)], near_sum[:, piece(k)])
        tally(1, saved[1, :, piece(k)], near_stage[:, piece(k)])
        tally(2, saved[2, :, piece(k)], far_own[:, piece(k)])
        @pl.when(k >= head)
        def _():
            send_far(k).wait_recv()
            far_sum[:, piece(k - head)] = far_total(k)

        send_near(k).wait_recv()
        near_sum[:, piece(k)] = (
            near_sum[:, piece(k)].astype(jnp.float32) + near_in[:, piece(k)].astype(jnp.float32)
        ).astype(jnp.bfloat16)

    @pl.loop(0, chunks)
    def _(k):
        pass_on(k).wait_recv()
        tally(3, saved[3, :, piece(k)], far_stage[:, piece(k)])

    for m in (1, 2, 3):
        part_to(m).start()

    @pl.loop(0, head)
    def _(k):
        to_head(k).wait_recv()
        near_sum[:, piece(k)] = (
            near_sum[:, piece(k)].astype(jnp.float32) + cross_head[:, piece(k)].astype(jnp.float32)
        ).astype(jnp.bfloat16)

    @pl.loop(0, chunks)
    def _(k):
        to_cross(k).wait_send()
        to_core(k).wait_send()
        pass_on(k).wait_send()
        send_far(k).wait_send()
        send_near(k).wait_send()

    @pl.loop(0, block_count)
    def _(b):
        @pl.when(b != block)
        def _():
            dispatch(b).wait_send()

    @pl.loop(0, head)
    def _(k):
        to_head(k).wait_send()

    for m in (1, 2, 3):
        to_dp(m).wait_send()
    for m in (1, 2, 3):
        part_to(m).wait_recv()
    part_sum[...] = (part[0] + part_in[1]) + (part_in[2] + part_in[3])
    for m in (1, 2, 3):
        part_to(m).wait_send()


def run_exchange(
    pad, id_rows, logit_rows, upstream, pick, pick_gate, slot_lane, hidden_saved, down_weight
):
    context_count = lax.axis_size("ctx")
    tensor_count = lax.axis_size("tp")
    block_count = context_count * tensor_count
    slots, hidden = hidden_saved.shape
    cols = down_weight.shape[1]
    chunks = hidden // chunk_width(slots, hidden)
    head_width = head_chunks(chunks) * (hidden // chunks)
    bf16, f32 = jnp.bfloat16, jnp.float32
    vmem = pl.BlockSpec(memory_space=pltpu.VMEM)
    dma = pltpu.SemaphoreType.DMA
    return pl.pallas_call(
        functools.partial(
            exchange, (context_count, tensor_count, block_count // EXPERTS)
        ),
        out_shape=[
            jax.ShapeDtypeStruct((slots, hidden - head_width), bf16),
            jax.ShapeDtypeStruct((slots, hidden), bf16),
            jax.ShapeDtypeStruct((4, slots, hidden), bf16),
            jax.ShapeDtypeStruct((4 * slots, cols), bf16),
            jax.ShapeDtypeStruct((slots, LANES), f32),
            jax.ShapeDtypeStruct((slots, LANES), f32),
        ],
        in_specs=[vmem] * 6 + [pl.BlockSpec(memory_space=pl.ANY)] * 2,
        out_specs=[vmem] * 6,
        scratch_shapes=[
            pltpu.VMEM((EXPERTS, pad, cols), bf16),
            pltpu.VMEM((block_count, pad, cols), bf16),
            pltpu.VMEM((3, slots, cols + LANES), bf16),
            pltpu.VMEM((4, slots, cols + LANES), bf16),
            pltpu.VMEM((hidden, cols), bf16),
            pltpu.VMEM((4 * slots, cols), bf16),
            pltpu.VMEM((slots, hidden), bf16),
            pltpu.VMEM((slots, hidden), bf16),
            pltpu.VMEM((slots, hidden), bf16),
            pltpu.VMEM((slots, hidden), bf16),
            pltpu.VMEM((slots, hidden), bf16),
            pltpu.VMEM((4, slots, LANES), f32),
            pltpu.VMEM((4, slots, LANES), f32),
            pltpu.VMEM((slots, head_width), bf16),
            pltpu.VMEM((slots, head_width), bf16),
            dma((block_count,)),
            dma((block_count,)),
            dma((4,)),
            dma((4,)),
            dma((4,)),
            dma((4,)),
            dma((head_chunks(chunks),)),
            dma((head_chunks(chunks),)),
        ]
        + [dma((chunks,))] * 11
        + [dma],
        compiler_params=pltpu.CompilerParams(
            collective_id=0, has_side_effects=True, vmem_limit_bytes=60 * 1024 * 1024
        ),
        cost_estimate=pl.CostEstimate(
            flops=8 * slots * hidden * cols, bytes_accessed=2 * hidden * cols, transcendentals=0
        ),
    )(id_rows, logit_rows, upstream, pick, pick_gate, slot_lane, hidden_saved, down_weight)


def local(upstream, router_logits, expert_ids, hidden_saved, down_weight):
    token_count, feature_cols = upstream.shape
    dp_count = lax.axis_size("dp")
    tensor_count = lax.axis_size("tp")
    context_count = lax.axis_size("ctx")
    block_count = context_count * tensor_count
    slots = hidden_saved.shape[0]
    capacity = slots // context_count
    group_size = block_count // EXPERTS
    pad = -(-(capacity + 1) // 16) * 16
    assert dp_count == 4 and tensor_count == dp_count
    assert capacity <= LANES and token_count == LANES

    joined = 4 if context_count % 4 == 0 else context_count
    index = np.arange(joined * capacity)
    first = (index // capacity) * pad
    columns = np.arange(joined * pad)[None, :]
    pick = ((first + index % capacity)[:, None] == columns).astype(jnp.bfloat16)
    pick_gate = ((first + capacity)[:, None] == columns).astype(jnp.bfloat16)
    slot_lane = ((index % capacity)[:, None] == np.arange(LANES)[None, :]).astype(np.float32)

    far_sum, near_sum, saved, weighted, gate_own, part = run_exchange(
        pad,
        expert_ids.T,
        router_logits.T,
        upstream,
        pick,
        pick_gate,
        slot_lane,
        hidden_saved,
        down_weight,
    )
    cross = swap(far_sum, 2)

    down_grad = lax.dot_general(
        saved.reshape(4 * slots, -1),
        weighted,
        (((0,), (0,)), ((), ())),
        preferred_element_type=jnp.float32,
    ).astype(jnp.bfloat16)

    part, expert_ids, router_logits, down_grad = lax.optimization_barrier(
        (part, expert_ids, router_logits, down_grad)
    )
    part = part.sum(axis=1)
    outgoing = jnp.broadcast_to(
        part.reshape(context_count, 1, capacity), (context_count, tensor_count, capacity)
    ).reshape(block_count, capacity)
    returned = lax.all_to_all(outgoing, ("ctx", "tp"), split_axis=0, concat_axis=0, tiled=True)
    expert_sums = returned.reshape(EXPERTS, group_size, capacity).sum(axis=1)
    gates = 1.0 / (1.0 + jnp.exp(router_logits[:, ::-1] - router_logits))
    onehot = (expert_ids[:, :, None] == jnp.arange(EXPERTS, dtype=jnp.int32)).astype(jnp.float32)
    number = jnp.arange(token_count, dtype=jnp.int32)
    prior = lax.dot_general(
        (number[:, None] > number[None, :]).astype(jnp.bfloat16),
        onehot.sum(axis=1).astype(jnp.bfloat16),
        (((1,), (0,)), ((), ())),
        preferred_element_type=jnp.float32,
    )
    slot = jnp.sum(onehot * prior[:, None, :], axis=2).astype(jnp.int32)
    at_slot = slot[:, :, None] == jnp.arange(capacity, dtype=jnp.int32)
    of_route = jnp.sum(onehot[:, :, :, None] * expert_sums[None, None], axis=2)
    route_grad = jnp.sum(jnp.where(at_slot, of_route, 0.0), axis=2)
    logit_grad = gates * (route_grad - jnp.sum(gates * route_grad, axis=1, keepdims=True))

    cross = jnp.pad(cross, ((0, 0), (near_sum.shape[1] - cross.shape[1], 0)))
    proj = near_sum.astype(jnp.float32) + cross.astype(jnp.float32)
    hidden_grad = (gate_own[:, :1] * proj).astype(jnp.bfloat16)
    return (hidden_grad, down_grad, logit_grad)


def solution(mesh):
    in_specs = (
        P(("dp", "ctx"), "tp"),
        P(("dp", "ctx"), None),
        P(("dp", "ctx"), None),
        P("dp", ("ctx", "tp")),
        P(("ctx", "tp"), "dp"),
    )
    out_specs = (P("dp", ("ctx", "tp")), P(("ctx", "tp"), "dp"), P(("dp", "ctx"), None))
    return jax.shard_map(local, mesh=mesh, in_specs=in_specs, out_specs=out_specs, check_vma=False)
```

```python
import functools

import jax
import jax.numpy as jnp
import numpy as np
from jax import lax
from jax.experimental import pallas as pl
from jax.experimental.pallas import tpu as pltpu
from jax.sharding import PartitionSpec as P

EXPERTS = 8
TOP = 2
LANES = 128
MESH = pl.DeviceIdType.MESH


def swap(value, distance):
    count = lax.axis_size("dp")
    return lax.ppermute(value, "dp", [(i, i ^ distance) for i in range(count)])


def chunk_width(slots, hidden):
    return min(1024 if slots <= 256 else 128, hidden)


def head_chunks(chunks):
    return chunks // 4


def exchange(
    sizes,
    id_rows,
    logit_rows,
    upstream,
    pick,
    pick_gate,
    slot_lane,
    saved_in,
    weight_in,
    far_sum,
    near_sum,
    saved_out,
    weighted,
    gate_out,
    part_sum,
    packed,
    recv,
    leaving,
    landing,
    weight,
    rows,
    far_own,
    far_stage,
    near_stage,
    far_in,
    near_in,
    part,
    part_in,
    saved,
    far_head,
    cross_head,
    disp_send,
    disp_recv,
    row_send,
    row_recv,
    part_send,
    part_recv,
    head_send,
    head_recv,
    cross_send,
    cross_recv,
    core_send,
    core_recv,
    pass_send,
    pass_recv,
    far_send,
    far_recv,
    near_send,
    near_recv,
    weight_sem,
    out_sem,
    own_sem,
):
    context_count, tensor_count, group_size = sizes
    block_count = context_count * tensor_count
    tokens, cols = upstream.shape
    slots = saved.shape[1]
    capacity = slots // context_count
    hidden = saved.shape[2]
    width = chunk_width(slots, hidden)
    chunks = hidden // width
    early = chunks * 5 // 8
    head = head_chunks(chunks)
    head_width = head * width
    pad = packed.shape[1]
    me = lax.axis_index("dp")
    ctx = lax.axis_index("ctx")
    tp = lax.axis_index("tp")
    mate = me + 1 - 2 * (me % 2)
    cross = me + 2 - 4 * ((me // 2) % 2)
    order = (me, mate, cross, cross + 1 - 2 * (cross % 2))
    block = ctx * tensor_count + tp

    def piece(k):
        return pl.ds(pl.multiple_of(k * width, width), width)

    def load(k):
        return pltpu.make_async_copy(
            weight_in.at[piece(k), :], weight.at[piece(k), :], weight_sem.at[k]
        )

    def write_out(k):
        return pltpu.make_async_copy(
            saved.at[:, :, piece(k)], saved_out.at[:, :, piece(k)], out_sem.at[k]
        )

    own = pltpu.make_async_copy(saved_in, saved.at[0], own_sem)

    barrier = pltpu.get_barrier_semaphore()

    @pl.loop(0, block_count)
    def _(b):
        @pl.when(b != block)
        def _():
            pl.semaphore_signal(
                barrier,
                inc=1,
                device_id=(me, b // tensor_count, b % tensor_count),
                device_id_type=MESH,
            )

    for other in order[1:]:
        pl.semaphore_signal(barrier, inc=1, device_id=(other, ctx, tp), device_id_type=MESH)

    @pl.loop(0, chunks)
    def _(k):
        load(k).start()

    own.start()

    f32, bf16 = jnp.float32, jnp.bfloat16
    token = lax.broadcasted_iota(jnp.int32, (tokens, tokens), 0)
    lane = lax.broadcasted_iota(jnp.int32, (tokens, tokens), 1)
    lane_value = lane.astype(f32)

    def column(line):
        return jnp.sum(jnp.where(token == lane, line, 0.0), axis=1, keepdims=True)

    experts = [column(id_rows[k : k + 1, :].astype(f32)) for k in range(TOP)]
    logits = [column(logit_rows[k : k + 1, :]) for k in range(TOP)]
    gates = [
        (1.0 / (1.0 + jnp.exp(logits[1 - k] - logits[k]))).astype(bf16).astype(f32)
        for k in range(TOP)
    ]
    named = [jnp.where(expert == lane_value, 1.0, 0.0) for expert in experts]
    prior = jnp.dot(
        jnp.where(lane < token, 1.0, 0.0).astype(bf16),
        (named[0] + named[1]).astype(bf16),
        preferred_element_type=f32,
    )
    slot = [jnp.sum(prior * one, axis=1, keepdims=True) for one in named]
    wide = lax.broadcasted_iota(jnp.int32, (tokens, EXPERTS * pad), 1).astype(f32)
    place = sum(
        jnp.where(experts[k] * float(pad) + slot[k] == wide, 1.0, 0.0) for k in range(TOP)
    )
    sorted_rows = lax.dot_general(
        place.astype(bf16), upstream[...], (((0,), (0,)), ((), ())), preferred_element_type=f32
    )
    gate_line = lax.broadcasted_iota(jnp.int32, (pad, LANES), 0) == capacity
    at_slot = [jnp.where(slot[k] == lane_value, gates[k], 0.0) for k in range(TOP)]
    for e in range(EXPERTS):
        line = sum(
            jnp.sum(jnp.where(experts[k] == float(e), at_slot[k], 0.0), axis=0, keepdims=True)
            for k in range(TOP)
        )
        found = sorted_rows[e * pad : (e + 1) * pad]
        packed[e, :, :LANES] = jnp.where(gate_line, line, found[:, :LANES]).astype(bf16)
        packed[e, :, LANES:] = found[:, LANES:].astype(bf16)

    pl.semaphore_wait(barrier, block_count - 1 + len(order) - 1)

    def dispatch(b):
        return pltpu.make_async_remote_copy(
            src_ref=packed.at[b // group_size],
            dst_ref=recv.at[block],
            send_sem=disp_send.at[b],
            recv_sem=disp_recv.at[block],
            device_id=(me, b // tensor_count, b % tensor_count),
            device_id_type=MESH,
        )

    def arrival(b):
        return pltpu.make_async_remote_copy(
            src_ref=packed.at[0],
            dst_ref=recv.at[b],
            send_sem=disp_send.at[0],
            recv_sem=disp_recv.at[b],
            device_id=(me, b // tensor_count, b % tensor_count),
            device_id_type=MESH,
        )

    def remote(src, dst, send, recv_sem, k, device):
        return pltpu.make_async_remote_copy(
            src_ref=src,
            dst_ref=dst,
            send_sem=send.at[k],
            recv_sem=recv_sem.at[k],
            device_id=(device, ctx, tp),
            device_id_type=MESH,
        )

    def to_dp(m):
        return remote(leaving.at[m - 1], landing.at[m], row_send, row_recv, m, order[m])

    def part_to(m):
        return remote(part.at[m], part_in.at[m], part_send, part_recv, m, order[m])

    def to_cross(k):
        return remote(
            saved_in.at[:, piece(k)], saved.at[2, :, piece(k)], cross_send, cross_recv, k, cross
        )

    def to_core(k):
        return remote(
            saved_in.at[:, piece(k)], saved.at[1, :, piece(k)], core_send, core_recv, k, mate
        )

    def pass_on(k):
        return remote(
            saved.at[2, :, piece(k)], saved.at[3, :, piece(k)], pass_send, pass_recv, k, mate
        )

    def send_far(k):
        return remote(
            far_stage.at[:, piece(k)], far_in.at[:, piece(k)], far_send, far_recv, k, mate
        )

    def send_near(k):
        return remote(
            near_stage.at[:, piece(k)], near_in.at[:, piece(k)], near_send, near_recv, k, mate
        )

    @pl.loop(1, block_count)
    def _(j):
        dispatch((block + j) % block_count).start()

    @pl.loop(0, early)
    def _(k):
        to_cross(k).start()

    recv[block] = packed[block // group_size]
    part[...] = jnp.zeros_like(part)

    @pl.loop(0, block_count)
    def _(b):
        @pl.when(b != block)
        def _():
            arrival(b).wait_recv()

    joined = pick.shape[1] // pad
    spans = [
        (first, pl.ds(first * capacity, joined * capacity))
        for first in range(0, context_count, joined)
    ]

    def block_rows(first, t):
        return jnp.concatenate(
            [recv[(first + c) * tensor_count + t] for c in range(joined)], axis=0
        )

    for first, span in spans:
        gate_lanes = jnp.dot(
            pick_gate[...], block_rows(first, 0)[:, :LANES], preferred_element_type=f32
        )
        gate = jnp.sum(gate_lanes * slot_lane[...], axis=1, keepdims=True)
        gate_out[span, :] = jnp.broadcast_to(gate, (joined * capacity, LANES))
    for m in (3, 2, 1, 0):
        there = leaving.at[m - 1] if m else landing.at[0]
        for first, span in spans:
            value = jnp.dot(pick[...], block_rows(first, order[m]), preferred_element_type=f32)
            there[span, :cols] = value.astype(bf16)
            there[span, cols:] = gate_out[span, :].astype(bf16)
        if m:
            to_dp(m).start()

    @pl.loop(early, chunks)
    def _(k):
        to_cross(k).start()

    @pl.loop(0, chunks)
    def _(k):
        to_core(k).start()

    for m in (1, 2, 3):
        to_dp(m).wait_recv()
    if slots % 16 == 0:
        pieces = [[(m, span)] for m in range(4) for _, span in spans]
    else:
        pieces = [[(m, pl.ds(0, slots)) for m in range(4)]]
    start = 0
    for group in pieces:
        row_values = jnp.concatenate(
            [landing[m, span, :cols].astype(f32) for m, span in group], axis=0
        )
        gate_column = jnp.concatenate(
            [landing[m, span, cols:].astype(f32)[:, :1] for m, span in group], axis=0
        )
        there = pl.ds(start, row_values.shape[0])
        rows[there, :] = row_values.astype(bf16)
        weighted[there, :] = (gate_column * row_values).astype(bf16)
        start += row_values.shape[0]

    @pl.loop(0, chunks)
    def _(k):
        load(k).wait()
        proj = lax.dot_general(
            rows[...],
            weight[piece(k), :],
            (((1,), (1,)), ((), ())),
            preferred_element_type=jnp.float32,
        )
        near_sum[:, piece(k)] = proj[:slots].astype(jnp.bfloat16)
        near_stage[:, piece(k)] = proj[slots : 2 * slots].astype(jnp.bfloat16)
        far_own[:, piece(k)] = proj[2 * slots : 3 * slots].astype(jnp.bfloat16)
        far_stage[:, piece(k)] = proj[3 * slots :].astype(jnp.bfloat16)
        send_far(k).start()
        send_near(k).start()

    def far_total(k):
        return (
            far_own[:, piece(k)].astype(jnp.float32) + far_in[:, piece(k)].astype(jnp.float32)
        ).astype(jnp.bfloat16)

    def to_head(k):
        return remote(
            far_head.at[:, piece(k)], cross_head.at[:, piece(k)], head_send, head_recv, k, cross
        )

    @pl.loop(0, head)
    def _(k):
        send_far(k).wait_recv()
        far_head[:, piece(k)] = far_total(k)
        to_head(k).start()

    own.wait()

    def tally(m, left, right):
        product = left.astype(jnp.float32) * right.astype(jnp.float32)
        total = product[:, :LANES]
        for j in range(1, width // LANES):
            total = total + product[:, j * LANES : (j + 1) * LANES]
        part[m] += total

    @pl.loop(0, chunks)
    def _(k):
        to_cross(k).wait_recv()
        pass_on(k).start()
        to_core(k).wait_recv()
        tally(0, saved[0, :, piece(k)], near_sum[:, piece(k)])
        tally(1, saved[1, :, piece(k)], near_stage[:, piece(k)])
        tally(2, saved[2, :, piece(k)], far_own[:, piece(k)])
        @pl.when(k >= head)
        def _():
            send_far(k).wait_recv()
            far_sum[:, piece(k - head)] = far_total(k)

        send_near(k).wait_recv()
        near_sum[:, piece(k)] = (
            near_sum[:, piece(k)].astype(jnp.float32) + near_in[:, piece(k)].astype(jnp.float32)
        ).astype(jnp.bfloat16)

    @pl.loop(0, chunks)
    def _(k):
        pass_on(k).wait_recv()
        write_out(k).start()
        tally(3, saved[3, :, piece(k)], far_stage[:, piece(k)])

    for m in (1, 2, 3):
        part_to(m).start()

    @pl.loop(0, head)
    def _(k):
        to_head(k).wait_recv()
        near_sum[:, piece(k)] = (
            near_sum[:, piece(k)].astype(jnp.float32) + cross_head[:, piece(k)].astype(jnp.float32)
        ).astype(jnp.bfloat16)

    @pl.loop(0, chunks)
    def _(k):
        write_out(k).wait()
        to_cross(k).wait_send()
        to_core(k).wait_send()
        pass_on(k).wait_send()
        send_far(k).wait_send()
        send_near(k).wait_send()

    @pl.loop(0, block_count)
    def _(b):
        @pl.when(b != block)
        def _():
            dispatch(b).wait_send()

    @pl.loop(0, head)
    def _(k):
        to_head(k).wait_send()

    for m in (1, 2, 3):
        to_dp(m).wait_send()
    for m in (1, 2, 3):
        part_to(m).wait_recv()
    part_sum[...] = (part[0] + part_in[1]) + (part_in[2] + part_in[3])
    for m in (1, 2, 3):
        part_to(m).wait_send()


def run_exchange(
    pad, id_rows, logit_rows, upstream, pick, pick_gate, slot_lane, hidden_saved, down_weight
):
    context_count = lax.axis_size("ctx")
    tensor_count = lax.axis_size("tp")
    block_count = context_count * tensor_count
    slots, hidden = hidden_saved.shape
    cols = down_weight.shape[1]
    chunks = hidden // chunk_width(slots, hidden)
    head_width = head_chunks(chunks) * (hidden // chunks)
    bf16, f32 = jnp.bfloat16, jnp.float32
    vmem = pl.BlockSpec(memory_space=pltpu.VMEM)
    dma = pltpu.SemaphoreType.DMA
    return pl.pallas_call(
        functools.partial(
            exchange, (context_count, tensor_count, block_count // EXPERTS)
        ),
        out_shape=[
            jax.ShapeDtypeStruct((slots, hidden - head_width), bf16),
            jax.ShapeDtypeStruct((slots, hidden), bf16),
            jax.ShapeDtypeStruct((4, slots, hidden), bf16),
            jax.ShapeDtypeStruct((4 * slots, cols), bf16),
            jax.ShapeDtypeStruct((slots, LANES), f32),
            jax.ShapeDtypeStruct((slots, LANES), f32),
        ],
        in_specs=[vmem] * 6 + [pl.BlockSpec(memory_space=pl.ANY)] * 2,
        out_specs=[vmem] * 2 + [pl.BlockSpec(memory_space=pl.ANY)] + [vmem] * 3,
        scratch_shapes=[
            pltpu.VMEM((EXPERTS, pad, cols), bf16),
            pltpu.VMEM((block_count, pad, cols), bf16),
            pltpu.VMEM((3, slots, cols + LANES), bf16),
            pltpu.VMEM((4, slots, cols + LANES), bf16),
            pltpu.VMEM((hidden, cols), bf16),
            pltpu.VMEM((4 * slots, cols), bf16),
            pltpu.VMEM((slots, hidden), bf16),
            pltpu.VMEM((slots, hidden), bf16),
            pltpu.VMEM((slots, hidden), bf16),
            pltpu.VMEM((slots, hidden), bf16),
            pltpu.VMEM((slots, hidden), bf16),
            pltpu.VMEM((4, slots, LANES), f32),
            pltpu.VMEM((4, slots, LANES), f32),
            pltpu.VMEM((4, slots, hidden), bf16),
            pltpu.VMEM((slots, head_width), bf16),
            pltpu.VMEM((slots, head_width), bf16),
            dma((block_count,)),
            dma((block_count,)),
            dma((4,)),
            dma((4,)),
            dma((4,)),
            dma((4,)),
            dma((head_chunks(chunks),)),
            dma((head_chunks(chunks),)),
        ]
        + [dma((chunks,))] * 12
        + [dma],
        compiler_params=pltpu.CompilerParams(
            collective_id=0, has_side_effects=True, vmem_limit_bytes=60 * 1024 * 1024
        ),
        cost_estimate=pl.CostEstimate(
            flops=8 * slots * hidden * cols, bytes_accessed=2 * hidden * cols, transcendentals=0
        ),
    )(id_rows, logit_rows, upstream, pick, pick_gate, slot_lane, hidden_saved, down_weight)


def gradient_block(saved, weighted, out):
    out[...] = lax.dot_general(
        saved[...], weighted[...], (((0,), (0,)), ((), ())), preferred_element_type=jnp.float32
    ).astype(jnp.bfloat16)


def weight_gradient(saved, weighted):
    depth, hidden = saved.shape
    cols = weighted.shape[1]
    block = min(1024 if depth <= 1024 else 256, hidden)
    return pl.pallas_call(
        gradient_block,
        grid=(hidden // block,),
        out_shape=jax.ShapeDtypeStruct((hidden, cols), jnp.bfloat16),
        in_specs=[
            pl.BlockSpec((depth, block), lambda i: (0, i)),
            pl.BlockSpec((depth, cols), lambda i: (0, 0)),
        ],
        out_specs=pl.BlockSpec((block, cols), lambda i: (i, 0)),
        compiler_params=pltpu.CompilerParams(vmem_limit_bytes=60 * 1024 * 1024),
        cost_estimate=pl.CostEstimate(
            flops=2 * depth * hidden * cols,
            bytes_accessed=2 * (depth * hidden + depth * cols + hidden * cols),
            transcendentals=0,
        ),
    )(saved, weighted)


def local(upstream, router_logits, expert_ids, hidden_saved, down_weight):
    token_count, feature_cols = upstream.shape
    dp_count = lax.axis_size("dp")
    tensor_count = lax.axis_size("tp")
    context_count = lax.axis_size("ctx")
    block_count = context_count * tensor_count
    slots = hidden_saved.shape[0]
    capacity = slots // context_count
    group_size = block_count // EXPERTS
    pad = -(-(capacity + 1) // 16) * 16
    assert dp_count == 4 and tensor_count == dp_count
    assert capacity <= LANES and token_count == LANES

    joined = 4 if context_count % 4 == 0 else context_count
    index = np.arange(joined * capacity)
    first = (index // capacity) * pad
    columns = np.arange(joined * pad)[None, :]
    pick = ((first + index % capacity)[:, None] == columns).astype(jnp.bfloat16)
    pick_gate = ((first + capacity)[:, None] == columns).astype(jnp.bfloat16)
    slot_lane = ((index % capacity)[:, None] == np.arange(LANES)[None, :]).astype(np.float32)

    far_sum, near_sum, saved, weighted, gate_own, part = run_exchange(
        pad,
        expert_ids.T,
        router_logits.T,
        upstream,
        pick,
        pick_gate,
        slot_lane,
        hidden_saved,
        down_weight,
    )
    cross = swap(far_sum, 2)

    down_grad = weight_gradient(saved.reshape(4 * slots, -1), weighted)

    part, expert_ids, router_logits, down_grad = lax.optimization_barrier(
        (part, expert_ids, router_logits, down_grad)
    )
    part = part.sum(axis=1)
    outgoing = jnp.broadcast_to(
        part.reshape(context_count, 1, capacity), (context_count, tensor_count, capacity)
    ).reshape(block_count, capacity)
    returned = lax.all_to_all(outgoing, ("ctx", "tp"), split_axis=0, concat_axis=0, tiled=True)
    expert_sums = returned.reshape(EXPERTS, group_size, capacity).sum(axis=1)
    gates = 1.0 / (1.0 + jnp.exp(router_logits[:, ::-1] - router_logits))
    onehot = (expert_ids[:, :, None] == jnp.arange(EXPERTS, dtype=jnp.int32)).astype(jnp.float32)
    number = jnp.arange(token_count, dtype=jnp.int32)
    prior = lax.dot_general(
        (number[:, None] > number[None, :]).astype(jnp.bfloat16),
        onehot.sum(axis=1).astype(jnp.bfloat16),
        (((1,), (0,)), ((), ())),
        preferred_element_type=jnp.float32,
    )
    slot = jnp.sum(onehot * prior[:, None, :], axis=2).astype(jnp.int32)
    at_slot = slot[:, :, None] == jnp.arange(capacity, dtype=jnp.int32)
    of_route = jnp.sum(onehot[:, :, :, None] * expert_sums[None, None], axis=2)
    route_grad = jnp.sum(jnp.where(at_slot, of_route, 0.0), axis=2)
    logit_grad = gates * (route_grad - jnp.sum(gates * route_grad, axis=1, keepdims=True))

    cross = jnp.pad(cross, ((0, 0), (near_sum.shape[1] - cross.shape[1], 0)))
    proj = near_sum.astype(jnp.float32) + cross.astype(jnp.float32)
    hidden_grad = (gate_own[:, :1] * proj).astype(jnp.bfloat16)
    return (hidden_grad, down_grad, logit_grad)


def solution(mesh):
    in_specs = (
        P(("dp", "ctx"), "tp"),
        P(("dp", "ctx"), None),
        P(("dp", "ctx"), None),
        P("dp", ("ctx", "tp")),
        P(("ctx", "tp"), "dp"),
    )
    out_specs = (P("dp", ("ctx", "tp")), P(("ctx", "tp"), "dp"), P(("dp", "ctx"), None))
    return jax.shard_map(local, mesh=mesh, in_specs=in_specs, out_specs=out_specs, check_vma=False)
```
